32 devices in a mesh: rows: 16 (over z, y, core), rep: 2 (over x).
Axes of the slice: x: 2, y: 2, z: 4, core: 2. Of those that a mesh axis runs over, the one named last changes fastest.
Arguments:
- embeddings: bfloat16 [11264, 1024], P(('rows', 'rep')), may hold values from -6 to 6
- owner_ids: int32 [11264, 1], P(('rows', 'rep')), may hold values from 0 to 15; in each aligned block of 352 rows (0 to 351, 352 to 703, ...) at most 64 rows name the same one
- live_mask: int32 [11264], P(('rows', 'rep')), may hold values 0 or 1
Outputs:
- neighbour_means: bfloat16 [11264, 1024], P(('rows', 'rep'))
The draws below stay inside these ranges and needn't reach their ends.
Inputs may be any that keep to these rules, and one draw needn't show every extreme that they name: `owner_ids`: among the rows of one device, at most 64 name the same owner, and in every draw some owner is named by exactly 64 of them.
All inputs are finite; a program needn't handle non-finite values. Where the reference program divides by a largest or mean magnitude, that divisor is 1e-20 or more. No bound on the sum of `live_mask` on one device may be relied on, other than what follows from the above.
Results may differ from the reference program's by a relative error of at most 0.0017.
The reference program's roundings to bfloat16 on the way count: a program that leaves them out, or rounds other values in their place, can miss the bound.
Values may be sent and summed in bfloat16 or wider, within the bound.
A program may use at most 64 MiB of HBM per device.

```python
import math
import jax
import jax.numpy as jnp
import numpy as np
from jax import lax

D = 1024
ROWS_DEV = 352
BUCKET = 1024
ITERS = 2
SLOT = 64
ROWS = 11264
N_ROWS = 16
N_REP = 2


def with_ends(values, rng, smallest, largest):
    spot = [jax.random.randint(jax.random.fold_in(rng, axis), (), 0, length) for axis, length in enumerate(values.shape)]
    main_axis = values.shape.index(max(values.shape))
    next_to = spot[:main_axis] + [(spot[main_axis] + 1) % values.shape[main_axis]] + spot[main_axis + 1:]
    return values.at[tuple(spot)].set(smallest).at[tuple(next_to)].set(largest)


def raised(values, stream_key, source, target, parts, factor):
    owner, partner = [(jnp.arange(values.shape[position]) // (values.shape[position] // parts)).reshape([-1 if axis == position else 1 for axis in range(values.ndim)]) for position in (source, target)]
    chosen = jax.random.permutation(stream_key, parts)[partner]
    strong = (owner == chosen) | (owner == (partner + parts // 2) % parts)
    return jnp.where(strong, factor * values, values)


def level_of(own_key, extent, pieces, low, high):
    level, own = 1.0, jax.random.fold_in(own_key, 6)
    for position, shards_of in pieces:
        steps = jnp.exp(jax.random.uniform(jax.random.fold_in(own, position), (shards_of,), jnp.float32, low / len(pieces), high / len(pieces)))
        level = level * jnp.repeat(steps, extent[position] // shards_of).reshape([-1 if axis == position else 1 for axis in range(len(extent))])
    return level


def routed_block(stream_key, own, number, rows, number_of, top, bound, lean):
    order = jax.random.permutation(stream_key, number_of)
    crowded, usual = shares(number_of, rows * top, bound, lean, True), shares(number_of, rows * top, bound, lean, False)
    places = jnp.arange(number_of)

    def named(lengths, rotation):
        used = int((lengths > 0).sum())
        fixed = max(1, used // 4)
        moved = fixed + (places - fixed + rotation * (used - fixed)) % max(1, number_of - fixed)
        return jnp.zeros((number_of,), jnp.int32).at[order[jnp.where(places < fixed, places, moved)]].set(jnp.asarray(lengths, jnp.int32))

    lengths = jnp.where(number % 4 == 0, named(crowded, number // 4), named(usual, number - number // 4 - 1))
    mixed = jax.random.permutation(jax.random.fold_in(own, 3), number_of)
    source_of, sink = mixed[0:number_of // 2 * 2:2], mixed[1:number_of // 2 * 2:2]
    slack = jnp.minimum(lengths[source_of] - 1, bound - lengths[sink]) // 2
    slack = jnp.where((source_of == order[0]) | (sink == order[0]) | (lengths[sink] == 0), 0, jnp.maximum(slack, 0))
    moved = jax.random.randint(jax.random.fold_in(own, 4), (number_of // 2,), 0, 1 << 20) % (slack + 1)
    lengths = lengths.at[source_of].add(-moved).at[sink].add(moved)
    labels = jnp.searchsorted(jnp.cumsum(lengths), jnp.arange(rows * top), side="right").astype(jnp.int32)
    grid = labels.reshape(top, rows).T
    grid = grid[jax.random.permutation(jax.random.fold_in(own, 1), rows)]
    rotation = jax.random.randint(jax.random.fold_in(own, 2), (rows, 1), 0, top)
    return jnp.take_along_axis(grid, (jnp.arange(top)[None, :] + rotation) % top, axis=1)


def shares(number_of, total, reach, skew, full):
    portions = [(1 << 20) // math.isqrt(rank ** skew) + 1 for rank in range(1, number_of + 1)]
    largest = reach if full else min(reach, max(-(-total // number_of), total * portions[0] // sum(portions)))
    least = 1 if total - largest >= number_of - 1 else 0
    holding, rest = [largest] + [least] * (number_of - 1), total - largest - least * (number_of - 1)
    while rest > 0:
        free = [i for i in range(1, number_of) if holding[i] < largest] or [i for i in range(1, number_of) if holding[i] < reach]
        whole, left = sum([portions[i] for i in free]), rest
        for i in free:
            extra = min(reach - holding[i], max(1, left * portions[i] // whole), rest)
            holding[i] = holding[i] + extra
            rest = rest - extra
    return np.array(holding)


def bell_draw_with(stream_key, extent, scale, limit, split, heavy, held_as=jnp.bfloat16):
    array = scale * jax.random.normal(stream_key, extent, jnp.float32)
    if split:
        array = array * level_of(stream_key, extent, split, -0.22, 0.18)
    return jnp.clip(raised(array, jax.random.fold_in(stream_key, 3), *heavy), -limit, limit).astype(held_as)


def setup_inputs(seed: int = 0) -> dict:
    seeds = jax.random.split(jax.random.key(seed), 4)
    embeddings = bell_draw_with(seeds[0], (ROWS, D), 1.0, 6.0, ((0, 32),), (0, 1, 32, 2.75))
    owner_ids_keys = jax.random.split(jax.random.fold_in(seeds[1], 1), ROWS // ROWS_DEV)
    owner_ids_turns = jax.random.permutation(jax.random.fold_in(seeds[1], 3), ROWS // ROWS_DEV)
    owner_ids = jax.vmap(lambda own, number: routed_block(jax.random.fold_in(seeds[1], 2), own, number, ROWS_DEV, N_ROWS, 1, SLOT, 2))(owner_ids_keys, owner_ids_turns).reshape((ROWS, 1))
    live_mask = with_ends((jax.random.randint(seeds[2], (ROWS,), 0, 8) < 7).astype(jnp.int32), jax.random.fold_in(seeds[2], 1), 0, 1)
    return {"embeddings": embeddings, "owner_ids": owner_ids, "live_mask": live_mask}


KERNEL_SCALE = 4.0
EPSILON = 1e-06
PRECISE = lax.Precision.HIGHEST

def block_positions(owner_block, owners, slot_cap):
    onehot = (owner_block[:, None] == jnp.arange(owners, dtype=jnp.int32)[None, :]).astype(jnp.int32)
    before = jnp.cumsum(onehot, axis=0) - onehot
    slot_rank = lax.optimization_barrier(jnp.sum(before * onehot, axis=1))
    return (owner_block * slot_cap + slot_rank).astype(jnp.int32)

def whiten(embedded, inverse_root):
    mapped = jnp.dot(embedded, inverse_root, preferred_element_type=jnp.float32)
    return (mapped * lax.rsqrt(lax.optimization_barrier(jnp.mean(mapped * mapped, axis=1, keepdims=True)) + EPSILON)).astype(jnp.bfloat16)

def bucket_means(members, alive):
    scores = jnp.dot(members, members.T, preferred_element_type=jnp.float32)
    weights = jnp.exp(KERNEL_SCALE * (scores / members.shape[1] - 1.0)) * alive[None, :]
    denominator = lax.optimization_barrier(jnp.sum(weights, axis=1, keepdims=True))
    summed = jnp.dot(weights.astype(jnp.bfloat16), members, preferred_element_type=jnp.float32)
    averaged = summed / jnp.where(alive[:, None] > 0, denominator, 1.0)
    normed = averaged * lax.rsqrt(lax.optimization_barrier(jnp.mean(averaged * averaged, axis=1, keepdims=True)) + EPSILON)
    return (normed * alive[:, None]).astype(jnp.bfloat16)

def reference(embeddings, owner_ids, live_mask):
    live_rows = live_mask.astype(jnp.bfloat16)
    masked = embeddings * live_rows[:, None]
    moment = jnp.dot(masked.T, masked, preferred_element_type=jnp.float32)
    y_iterate = moment / jnp.max(lax.optimization_barrier(jnp.sum(jnp.abs(moment), axis=1)))
    z_iterate = jnp.eye(D, dtype=jnp.float32)
    for iteration in range(ITERS):
        product = jnp.dot(z_iterate, y_iterate, precision=PRECISE)
        y_next = 0.5 * (3.0 * y_iterate - jnp.dot(product, y_iterate, precision=PRECISE))
        z_iterate = 0.5 * (3.0 * z_iterate - jnp.dot(product, z_iterate, precision=PRECISE))
        y_iterate = y_next
    inverse_root = z_iterate.astype(jnp.bfloat16)
    whitened = whiten(embeddings, inverse_root)
    devices_n = N_ROWS * N_REP
    total_rows = devices_n * ROWS_DEV
    blocks = owner_ids[:, 0].reshape(devices_n, ROWS_DEV).astype(jnp.int32)
    positions = lax.map(lambda owner_block: block_positions(owner_block, N_ROWS, SLOT), blocks)
    slot_rank = positions - blocks * SLOT
    source = jnp.arange(devices_n, dtype=jnp.int32)
    bucket_id = blocks * N_REP + (source % N_REP)[:, None]
    place = bucket_id * BUCKET + (source // N_REP)[:, None] * SLOT + slot_rank
    table = jnp.full((devices_n * BUCKET,), total_rows, jnp.int32)
    table = table.at[place.reshape(-1)].set(jnp.arange(total_rows, dtype=jnp.int32))
    padded = jnp.concatenate([whitened, jnp.zeros((1, D), jnp.bfloat16)], axis=0)
    alive_pad = jnp.concatenate([live_mask.astype(jnp.float32), jnp.zeros((1,), jnp.float32)])

    def visit(bucket_n, result):
        members_at = lax.dynamic_slice_in_dim(table, bucket_n * BUCKET, BUCKET)
        means = bucket_means(padded[members_at], alive_pad[members_at])
        return result.at[members_at].set(means, mode='drop')
    result = jnp.zeros((total_rows, D), jnp.bfloat16)
    return lax.fori_loop(0, devices_n, visit, result)
```

```python
import jax
import jax.numpy as jnp
from jax import lax
from jax.sharding import PartitionSpec as P

BUCKET = 1024
JOIN_ROWS = 8192
KERNEL_SCALE = 4.0
EPSILON = 1e-06
SPLIT = lax.Precision.HIGH
PRECISE = lax.Precision.HIGHEST


def block_positions(owner_block, owners, slot_cap):
    rows = owner_block.shape[0]
    same = owner_block[:, None] == owner_block[None, :]
    index = jnp.arange(rows, dtype=jnp.int32)
    earlier = index[None, :] < index[:, None]
    slot_rank = jnp.sum((same & earlier).astype(jnp.int32), axis=1)
    return owner_block * slot_cap + slot_rank


def whiten(embedded, inverse_root):
    mapped = jnp.dot(embedded, inverse_root, preferred_element_type=jnp.float32)
    return (mapped * lax.rsqrt(jnp.mean(mapped * mapped, axis=1, keepdims=True) + EPSILON)).astype(
        jnp.bfloat16
    )


def root_of(moment):
    y = moment / jnp.max(jnp.sum(jnp.abs(moment), axis=1))
    eye = jnp.eye(y.shape[0], dtype=jnp.float32)
    square = jnp.dot(y, y, precision=SPLIT)
    inner = 1.6875 * eye - 0.5625 * y + 0.0625 * square
    return (2.25 * eye - 2.4375 * y + jnp.dot(square, inner, precision=SPLIT)).astype(jnp.bfloat16)


def masked_means(queries, members, same, alive):
    scores = lax.dot_general(
        queries, members, (((1,), (1,)), ((), ())), preferred_element_type=jnp.float32
    )
    weights = jnp.where(same, jnp.exp(KERNEL_SCALE * (scores / members.shape[1] - 1.0)), 0.0)
    denominator = jnp.sum(weights, axis=1, keepdims=True)
    summed = jnp.dot(weights.astype(jnp.bfloat16), members, preferred_element_type=jnp.float32)
    averaged = summed / jnp.where(alive[:, None] > 0, denominator, 1.0)
    normed = averaged * lax.rsqrt(jnp.mean(averaged * averaged, axis=1, keepdims=True) + EPSILON)
    return (normed * alive[:, None]).astype(jnp.bfloat16)


def spread(values, positions, slots_all):
    return jnp.zeros((slots_all,) + values.shape[1:], values.dtype).at[positions].set(values)


def by_exchange(embeddings, owner_ids, live_mask):
    rows_here, columns = embeddings.shape
    owners = lax.axis_size("rows")
    slot_cap = BUCKET // owners
    positions = block_positions(owner_ids[:, 0], owners, slot_cap)
    live_rows = live_mask.astype(jnp.bfloat16)
    masked = embeddings * live_rows[:, None]
    partial_moment = lax.dot_general(
        masked, masked, (((0,), (0,)), ((), ())), preferred_element_type=jnp.float32
    )
    inverse_root = root_of(lax.psum(partial_moment, ("rows", "rep")))
    whitened = whiten(embeddings, inverse_root)

    def swapped(values):
        return lax.all_to_all(values, "rows", split_axis=0, concat_axis=0, tiled=True)

    members = swapped(
        spread(whitened, positions, BUCKET).reshape(owners, slot_cap, columns)
    ).reshape(BUCKET, columns)
    alive = swapped(spread(live_rows, positions, BUCKET).reshape(owners, slot_cap))
    alive = alive.reshape(BUCKET).astype(jnp.float32)
    means = masked_means(members, members, alive[None, :] > 0, alive)
    returned = swapped(means.reshape(owners, slot_cap, columns))
    return returned.reshape(BUCKET, columns)[positions]


def by_gather(embeddings, owner_ids, live_mask):
    rows_here, columns = embeddings.shape
    owners = lax.axis_size("rows")
    key = jnp.where(live_mask > 0, owner_ids[:, 0], -1)
    keys = lax.all_gather(key, "rows", axis=0, tiled=True)
    everyone = lax.all_gather(embeddings, "rows", axis=0, tiled=True)
    share = columns // owners
    masked = everyone * (keys >= 0).astype(jnp.bfloat16)[:, None]
    own = lax.dynamic_slice_in_dim(masked, lax.axis_index("rows") * share, share, 1)
    part = lax.dot_general(own, masked, (((0,), (0,)), ((), ())), preferred_element_type=jnp.float32)
    part = lax.psum(part, "rep")
    moment = lax.all_gather(part, "rows", axis=0, tiled=True)
    whitened = whiten(everyone, root_of(moment))
    mine = lax.dynamic_slice_in_dim(whitened, lax.axis_index("rows") * rows_here, rows_here, 0)
    alive = (live_mask > 0).astype(jnp.float32)
    return masked_means(mine, whitened, owner_ids == keys[None, :], alive)


def solution(mesh):
    placed = (P(("rows", "rep"), None), P(("rows", "rep"), None), P(("rows", "rep")))

    def per_device(embeddings, owner_ids, live_mask):
        gathered = embeddings.shape[0] * mesh.shape["rows"]
        join = by_gather if gathered <= JOIN_ROWS else by_exchange
        return join(embeddings, owner_ids, live_mask)

    return jax.shard_map(
        per_device, mesh=mesh, in_specs=placed, out_specs=P(("rows", "rep"), None), check_vma=False
    )
```

```python
import functools

import jax
import jax.numpy as jnp
from jax import lax
from jax.experimental import pallas as pl
from jax.experimental.pallas import tpu as pltpu
from jax.sharding import PartitionSpec as P

BUCKET = 1024
JOIN_ROWS = 8192
KERNEL_SCALE = 4.0
EPSILON = 1e-06
SPLIT = lax.Precision.HIGH
PRECISE = lax.Precision.HIGHEST


def block_positions(owner_block, owners, slot_cap):
    rows = owner_block.shape[0]
    same = owner_block[:, None] == owner_block[None, :]
    index = jnp.arange(rows, dtype=jnp.int32)
    earlier = index[None, :] < index[:, None]
    slot_rank = jnp.sum((same & earlier).astype(jnp.int32), axis=1)
    return owner_block * slot_cap + slot_rank


def whiten(embedded, inverse_root):
    mapped = jnp.dot(embedded, inverse_root, preferred_element_type=jnp.float32)
    return (mapped * lax.rsqrt(jnp.mean(mapped * mapped, axis=1, keepdims=True) + EPSILON)).astype(
        jnp.bfloat16
    )


def root_of(moment):
    y = moment / jnp.max(jnp.sum(jnp.abs(moment), axis=1))
    eye = jnp.eye(y.shape[0], dtype=jnp.float32)
    square = jnp.dot(y, y, precision=SPLIT)
    inner = 1.6875 * eye - 0.5625 * y + 0.0625 * square
    return (2.25 * eye - 2.4375 * y + jnp.dot(square, inner, precision=SPLIT)).astype(jnp.bfloat16)


def masked_means(queries, members, same, alive):
    scores = lax.dot_general(
        queries, members, (((1,), (1,)), ((), ())), preferred_element_type=jnp.float32
    )
    weights = jnp.where(same, jnp.exp(KERNEL_SCALE * (scores / members.shape[1] - 1.0)), 0.0)
    denominator = jnp.sum(weights, axis=1, keepdims=True)
    summed = jnp.dot(weights.astype(jnp.bfloat16), members, preferred_element_type=jnp.float32)
    averaged = summed / jnp.where(alive[:, None] > 0, denominator, 1.0)
    normed = averaged * lax.rsqrt(jnp.mean(averaged * averaged, axis=1, keepdims=True) + EPSILON)
    return (normed * alive[:, None]).astype(jnp.bfloat16)


def spread(values, positions, slots_all):
    return jnp.zeros((slots_all,) + values.shape[1:], values.dtype).at[positions].set(values)


def by_exchange(embeddings, owner_ids, live_mask):
    rows_here, columns = embeddings.shape
    owners = lax.axis_size("rows")
    slot_cap = BUCKET // owners
    positions = block_positions(owner_ids[:, 0], owners, slot_cap)
    live_rows = live_mask.astype(jnp.bfloat16)
    masked = embeddings * live_rows[:, None]
    partial_moment = lax.dot_general(
        masked, masked, (((0,), (0,)), ((), ())), preferred_element_type=jnp.float32
    )
    inverse_root = root_of(lax.psum(partial_moment, ("rows", "rep")))
    whitened = whiten(embeddings, inverse_root)

    def swapped(values):
        return lax.all_to_all(values, "rows", split_axis=0, concat_axis=0, tiled=True)

    members = swapped(
        spread(whitened, positions, BUCKET).reshape(owners, slot_cap, columns)
    ).reshape(BUCKET, columns)
    alive = swapped(spread(live_rows, positions, BUCKET).reshape(owners, slot_cap))
    alive = alive.reshape(BUCKET).astype(jnp.float32)
    means = masked_means(members, members, alive[None, :] > 0, alive)
    returned = swapped(means.reshape(owners, slot_cap, columns))
    return returned.reshape(BUCKET, columns)[positions]


def gather_kernel(owners, reduced, chunks, *refs):
    if reduced:
        x_ref, out_ref, other, own, pair_sems, here_sem, z_send, z_recv, y_send, y_recv, c_send, c_recv = refs
    else:
        x_ref, out_ref, here_sem, z_send, z_recv, y_send, y_recv, c_send, c_recv = refs
    me = lax.axis_index("rows")
    core, y, z = me % 2, (me // 2) % 2, me // 4
    depth = owners // 4

    def at(z_, y_, core_):
        return z_ * 4 + y_ * 2 + core_

    beside, sibling = at(z, 1 - y, core), at(z, y, 1 - core)
    along = [at((z + d) % depth, y, core) for d in range(1, depth)]
    barrier = pltpu.get_barrier_semaphore()
    for peer in along + [beside, sibling]:
        pl.semaphore_signal(
            barrier, inc=1, device_id={"rows": peer}, device_id_type=pl.DeviceIdType.MESH
        )
    if reduced:
        across = {"rep": 1 - lax.axis_index("rep")}
        pl.semaphore_signal(
            barrier, inc=1, device_id=across, device_id_type=pl.DeviceIdType.MESH
        )
    pl.semaphore_wait(barrier, depth + 1 + int(reduced))

    source = x_ref
    if reduced:
        swap = pltpu.make_async_remote_copy(
            src_ref=x_ref,
            dst_ref=other,
            send_sem=pair_sems.at[0],
            recv_sem=pair_sems.at[1],
            device_id=across,
            device_id_type=pl.DeviceIdType.MESH,
        )
        swap.start()
        swap.wait()
        own[...] = x_ref[...] + other[...]
        source = own

    started = []

    def send(block, k, peer, send_sems, recv_sems, n, first=False):
        rows = pl.ds(*chunks[k])
        copy = pltpu.make_async_remote_copy(
            src_ref=source.at[rows] if first else out_ref.at[block, rows],
            dst_ref=out_ref.at[block, rows],
            send_sem=send_sems.at[n, k],
            recv_sem=recv_sems.at[n, k],
            device_id={"rows": peer},
            device_id_type=pl.DeviceIdType.MESH,
        )
        copy.start()
        started.append(copy)

    def arrived(block, k, recv_sems, n):
        rows = pl.ds(*chunks[k])
        place = out_ref.at[block, rows]
        pltpu.make_async_copy(place, place, recv_sems.at[n, k]).wait()

    here = pltpu.make_async_copy(source, out_ref.at[me], here_sem)
    here.start()
    order = sorted(range(1, depth), key=lambda d: min(d, depth - d))
    for k in range(len(chunks)):
        send(me, k, beside, y_send, y_recv, 0, True)
        for d in order:
            send(me, k, along[d - 1], z_send, z_recv, d - 1, True)
        send(me, k, sibling, c_send, c_recv, 0, True)
    for k in range(len(chunks)):
        for d in order:
            block = at((z + depth - d) % depth, y, core)
            arrived(block, k, z_recv, d - 1)
            send(block, k, beside, y_send, y_recv, d)
            send(block, k, sibling, c_send, c_recv, d)
    for d in [0] + order:
        for k in range(len(chunks)):
            block = at((z + depth - d) % depth, 1 - y, core)
            arrived(block, k, y_recv, d)
            send(block, k, sibling, c_send, c_recv, depth + d)
    for d in range(depth):
        for k in range(len(chunks)):
            arrived(at((z + depth - d) % depth, y, 1 - core), k, c_recv, d)
            arrived(at((z + depth - d) % depth, 1 - y, 1 - core), k, c_recv, depth + d)
    for copy in started:
        copy.wait_send()
    here.wait()


def plane_gather(block, owners, chunk, collective_id, reduced=False):
    rows = block.shape[0]
    chunks = [(start, min(chunk, rows - start)) for start in range(0, rows, chunk)]
    n, depth = len(chunks), owners // 4
    dma = pltpu.SemaphoreType.DMA
    scratch = [dma(())] + [
        dma((count, n)) for count in (depth - 1, depth - 1, depth, depth, 2 * depth, 2 * depth)
    ]
    if reduced:
        scratch = [
            pltpu.VMEM(block.shape, block.dtype),
            pltpu.VMEM(block.shape, block.dtype),
            dma((2,)),
        ] + scratch
    return pl.pallas_call(
        functools.partial(gather_kernel, owners, reduced, chunks),
        out_shape=jax.ShapeDtypeStruct((owners,) + block.shape, block.dtype),
        in_specs=[pl.BlockSpec(memory_space=pltpu.VMEM if reduced else pl.ANY)],
        out_specs=pl.BlockSpec(memory_space=pl.ANY),
        scratch_shapes=scratch,
        compiler_params=pltpu.CompilerParams(
            collective_id=collective_id, has_side_effects=True, vmem_limit_bytes=16 << 20
        ),
    )(block)


def whiten_kernel(x_ref, root_ref, out_ref):
    mapped = jnp.dot(x_ref[...], root_ref[...], preferred_element_type=jnp.float32)
    scale = lax.rsqrt(jnp.mean(mapped * mapped, axis=1, keepdims=True) + EPSILON)
    out_ref[...] = (mapped * scale).astype(jnp.bfloat16)


def whiten_rows(rows, root, tile):
    count, columns = rows.shape
    return pl.pallas_call(
        whiten_kernel,
        grid=(count // tile,),
        out_shape=jax.ShapeDtypeStruct(rows.shape, jnp.bfloat16),
        in_specs=[
            pl.BlockSpec((tile, columns), lambda i: (i, 0)),
            pl.BlockSpec((columns, columns), lambda i: (0, 0)),
        ],
        out_specs=pl.BlockSpec((tile, columns), lambda i: (i, 0)),
        compiler_params=pltpu.CompilerParams(vmem_limit_bytes=32 << 20),
    )(rows, root)


def by_gather(embeddings, owner_ids, live_mask):
    rows_here, columns = embeddings.shape
    owners = lax.axis_size("rows")
    key = jnp.where(live_mask > 0, owner_ids[:, 0], -1)
    extra = jnp.pad(key.astype(jnp.bfloat16)[None, :], ((0, 15), (0, columns - rows_here)))
    block = jnp.concatenate([embeddings, extra], axis=0)
    held = block.shape[0]
    blocks = plane_gather(block, owners, 96, 1)
    keys = blocks[:, rows_here, :rows_here].astype(jnp.int32)
    keys = jnp.pad(keys, ((0, 0), (0, held - rows_here)), constant_values=-1).reshape(-1)
    everyone = blocks.reshape(owners * held, columns)
    share = columns // owners
    live = (keys >= 0).astype(jnp.bfloat16)[:, None]
    own = lax.dynamic_slice_in_dim(everyone, lax.axis_index("rows") * share, share, 1) * live
    part = lax.dot_general(
        own, everyone, (((0,), (0,)), ((), ())), preferred_element_type=jnp.float32
    )
    moment = plane_gather(part, owners, 32, 2, True).reshape(columns, columns)
    whitened = whiten_rows(everyone, root_of(moment), held)
    mine = lax.dynamic_slice_in_dim(whitened, lax.axis_index("rows") * held, rows_here, 0)
    alive = (live_mask > 0).astype(jnp.float32)
    return masked_means(mine, whitened, owner_ids == keys[None, :], alive)


def solution(mesh):
    placed = (P(("rows", "rep"), None), P(("rows", "rep"), None), P(("rows", "rep")))

    def per_device(embeddings, owner_ids, live_mask):
        gathered = embeddings.shape[0] * mesh.shape["rows"]
        fits = gathered <= JOIN_ROWS and mesh.shape["rep"] == 2
        join = by_gather if fits else by_exchange
        return join(embeddings, owner_ids, live_mask)

    return jax.shard_map(
        per_device, mesh=mesh, in_specs=placed, out_specs=P(("rows", "rep"), None), check_vma=False
    )
```

```python
import functools

import jax
import jax.numpy as jnp
from jax import lax
from jax.experimental import pallas as pl
from jax.experimental.pallas import tpu as pltpu
from jax.sharding import PartitionSpec as P

BUCKET = 1024
JOIN_ROWS = 8192
KERNEL_SCALE = 4.0
EPSILON = 1e-06
SPLIT = lax.Precision.HIGH
PRECISE = lax.Precision.HIGHEST


def block_positions(owner_block, owners, slot_cap):
    rows = owner_block.shape[0]
    same = owner_block[:, None] == owner_block[None, :]
    index = jnp.arange(rows, dtype=jnp.int32)
    earlier = index[None, :] < index[:, None]
    slot_rank = jnp.sum((same & earlier).astype(jnp.int32), axis=1)
    return owner_block * slot_cap + slot_rank


def whiten(embedded, inverse_root):
    mapped = jnp.dot(embedded, inverse_root, preferred_element_type=jnp.float32)
    return (mapped * lax.rsqrt(jnp.mean(mapped * mapped, axis=1, keepdims=True) + EPSILON)).astype(
        jnp.bfloat16
    )


def root_of(moment):
    y = moment / jnp.max(jnp.sum(jnp.abs(moment), axis=1))
    eye = jnp.eye(y.shape[0], dtype=jnp.float32)
    square = jnp.dot(y, y, precision=SPLIT)
    inner = 1.6875 * eye - 0.5625 * y + 0.0625 * square
    return (2.25 * eye - 2.4375 * y + jnp.dot(square, inner, precision=SPLIT)).astype(jnp.bfloat16)


def masked_means(queries, members, same, alive):
    scores = lax.dot_general(
        queries, members, (((1,), (1,)), ((), ())), preferred_element_type=jnp.float32
    )
    weights = jnp.where(same, jnp.exp(KERNEL_SCALE * (scores / members.shape[1] - 1.0)), 0.0)
    denominator = jnp.sum(weights, axis=1, keepdims=True)
    summed = jnp.dot(weights.astype(jnp.bfloat16), members, preferred_element_type=jnp.float32)
    averaged = summed / jnp.where(alive[:, None] > 0, denominator, 1.0)
    normed = averaged * lax.rsqrt(jnp.mean(averaged * averaged, axis=1, keepdims=True) + EPSILON)
    return (normed * alive[:, None]).astype(jnp.bfloat16)


def spread(values, positions, slots_all):
    return jnp.zeros((slots_all,) + values.shape[1:], values.dtype).at[positions].set(values)


def by_exchange(embeddings, owner_ids, live_mask):
    rows_here, columns = embeddings.shape
    owners = lax.axis_size("rows")
    slot_cap = BUCKET // owners
    positions = block_positions(owner_ids[:, 0], owners, slot_cap)
    live_rows = live_mask.astype(jnp.bfloat16)
    masked = embeddings * live_rows[:, None]
    partial_moment = lax.dot_general(
        masked, masked, (((0,), (0,)), ((), ())), preferred_element_type=jnp.float32
    )
    inverse_root = root_of(lax.psum(partial_moment, ("rows", "rep")))
    whitened = whiten(embeddings, inverse_root)

    def swapped(values):
        return lax.all_to_all(values, "rows", split_axis=0, concat_axis=0, tiled=True)

    members = swapped(
        spread(whitened, positions, BUCKET).reshape(owners, slot_cap, columns)
    ).reshape(BUCKET, columns)
    alive = swapped(spread(live_rows, positions, BUCKET).reshape(owners, slot_cap))
    alive = alive.reshape(BUCKET).astype(jnp.float32)
    means = masked_means(members, members, alive[None, :] > 0, alive)
    returned = swapped(means.reshape(owners, slot_cap, columns))
    return returned.reshape(BUCKET, columns)[positions]


def gather_kernel(owners, reduced, chunks, *refs):
    if reduced:
        x_ref, out_ref, other, own, pair_sems, here_sem, z_send, z_recv, y_send, y_recv, c_send, c_recv = refs
    else:
        x_ref, out_ref, here_sem, z_send, z_recv, y_send, y_recv, c_send, c_recv = refs
    me = lax.axis_index("rows")
    core, y, z = me % 2, (me // 2) % 2, me // 4
    depth = owners // 4

    def at(z_, y_, core_):
        return z_ * 4 + y_ * 2 + core_

    beside, sibling = at(z, 1 - y, core), at(z, y, 1 - core)
    along = [at((z + d) % depth, y, core) for d in range(1, depth)]
    barrier = pltpu.get_barrier_semaphore()
    for peer in along + [beside, sibling]:
        pl.semaphore_signal(
            barrier, inc=1, device_id={"rows": peer}, device_id_type=pl.DeviceIdType.MESH
        )
    if reduced:
        across = {"rep": 1 - lax.axis_index("rep")}
        pl.semaphore_signal(
            barrier, inc=1, device_id=across, device_id_type=pl.DeviceIdType.MESH
        )
    pl.semaphore_wait(barrier, depth + 1 + int(reduced))

    source = x_ref
    if reduced:
        swap = pltpu.make_async_remote_copy(
            src_ref=x_ref,
            dst_ref=other,
            send_sem=pair_sems.at[0],
            recv_sem=pair_sems.at[1],
            device_id=across,
            device_id_type=pl.DeviceIdType.MESH,
        )
        swap.start()
        swap.wait()
        own[...] = x_ref[...] + other[...]
        source = own

    started = []

    def send(block, k, peer, send_sems, recv_sems, n, first=False):
        rows = pl.ds(*chunks[k])
        copy = pltpu.make_async_remote_copy(
            src_ref=source.at[rows] if first else out_ref.at[block, rows],
            dst_ref=out_ref.at[block, rows],
            send_sem=send_sems.at[n, k],
            recv_sem=recv_sems.at[n, k],
            device_id={"rows": peer},
            device_id_type=pl.DeviceIdType.MESH,
        )
        copy.start()
        started.append(copy)

    def arrived(block, k, recv_sems, n):
        rows = pl.ds(*chunks[k])
        place = out_ref.at[block, rows]
        pltpu.make_async_copy(place, place, recv_sems.at[n, k]).wait()

    here = pltpu.make_async_copy(source, out_ref.at[me], here_sem)
    here.start()
    order = sorted(range(1, depth), key=lambda d: min(d, depth - d))
    for k in range(len(chunks)):
        send(me, k, beside, y_send, y_recv, 0, True)
        for d in order:
            send(me, k, along[d - 1], z_send, z_recv, d - 1, True)
        send(me, k, sibling, c_send, c_recv, 0, True)
    for k in range(len(chunks)):
        for d in order:
            block = at((z + depth - d) % depth, y, core)
            arrived(block, k, z_recv, d - 1)
            send(block, k, beside, y_send, y_recv, d)
            send(block, k, sibling, c_send, c_recv, d)
    for d in [0] + order:
        for k in range(len(chunks)):
            block = at((z + depth - d) % depth, 1 - y, core)
            arrived(block, k, y_recv, d)
            send(block, k, sibling, c_send, c_recv, depth + d)
    for d in range(depth):
        for k in range(len(chunks)):
            arrived(at((z + depth - d) % depth, y, 1 - core), k, c_recv, d)
            arrived(at((z + depth - d) % depth, 1 - y, 1 - core), k, c_recv, depth + d)
    for copy in started:
        copy.wait_send()
    here.wait()


def plane_gather(block, owners, chunk, collective_id, reduced=False):
    rows = block.shape[0]
    chunks = [(start, min(chunk, rows - start)) for start in range(0, rows, chunk)]
    n, depth = len(chunks), owners // 4
    dma = pltpu.SemaphoreType.DMA
    scratch = [dma(())] + [
        dma((count, n)) for count in (depth - 1, depth - 1, depth, depth, 2 * depth, 2 * depth)
    ]
    if reduced:
        scratch = [
            pltpu.VMEM(block.shape, block.dtype),
            pltpu.VMEM(block.shape, block.dtype),
            dma((2,)),
        ] + scratch
    return pl.pallas_call(
        functools.partial(gather_kernel, owners, reduced, chunks),
        out_shape=jax.ShapeDtypeStruct((owners,) + block.shape, block.dtype),
        in_specs=[pl.BlockSpec(memory_space=pltpu.VMEM if reduced else pl.ANY)],
        out_specs=pl.BlockSpec(memory_space=pl.ANY),
        scratch_shapes=scratch,
        compiler_params=pltpu.CompilerParams(
            collective_id=collective_id, has_side_effects=True, vmem_limit_bytes=16 << 20
        ),
    )(block)


def whitened_block(rows, root):
    mapped = jnp.dot(rows, root, preferred_element_type=jnp.float32)
    scale = lax.rsqrt(jnp.mean(mapped * mapped, axis=1, keepdims=True) + EPSILON)
    return (mapped * scale).astype(jnp.bfloat16)


def join_kernel(own_ref, named_ref, alive_ref, root_ref, x_ref, key_ref, out_ref, query, total, norm):
    step = pl.program_id(0)

    @pl.when(step == 0)
    def _():
        query[...] = whitened_block(own_ref[...], root_ref[...])
        total[...] = jnp.zeros_like(total)
        norm[...] = jnp.zeros_like(norm)

    members = whitened_block(x_ref[0], root_ref[...])
    scores = lax.dot_general(
        query[...], members, (((1,), (1,)), ((), ())), preferred_element_type=jnp.float32
    )
    close = jnp.exp(KERNEL_SCALE * (scores * (1.0 / members.shape[1]) - 1.0))
    weights = jnp.where(named_ref[...] == key_ref[0], close, 0.0)
    norm[...] += jnp.sum(weights, axis=1, keepdims=True)
    total[...] += jnp.dot(
        weights.astype(jnp.bfloat16), members, preferred_element_type=jnp.float32
    )

    @pl.when(step == pl.num_programs(0) - 1)
    def _():
        alive = alive_ref[...]
        averaged = total[...] / jnp.where(alive > 0, norm[...], 1.0)
        scale = lax.rsqrt(jnp.mean(averaged * averaged, axis=1, keepdims=True) + EPSILON)
        out_ref[...] = (averaged * scale * alive).astype(jnp.bfloat16)


def join_rows(own, named, alive, root, blocks, keys):
    rows, columns = own.shape
    count, held, _ = blocks.shape

    def whole(shape):
        return pl.BlockSpec(shape, lambda i: (0, 0))

    return pl.pallas_call(
        join_kernel,
        grid=(count,),
        out_shape=jax.ShapeDtypeStruct(own.shape, jnp.bfloat16),
        in_specs=[
            whole(own.shape),
            whole(named.shape),
            whole(alive.shape),
            whole(root.shape),
            pl.BlockSpec((1, held, columns), lambda i: (i, 0, 0)),
            pl.BlockSpec((1, 1, held), lambda i: (i, 0, 0)),
        ],
        out_specs=whole(own.shape),
        scratch_shapes=[
            pltpu.VMEM((rows, columns), jnp.bfloat16),
            pltpu.VMEM((rows, columns), jnp.float32),
            pltpu.VMEM((rows, 1), jnp.float32),
        ],
        compiler_params=pltpu.CompilerParams(vmem_limit_bytes=40 << 20),
    )(own, named, alive, root, blocks, keys)


def by_gather(embeddings, owner_ids, live_mask):
    rows_here, columns = embeddings.shape
    owners = lax.axis_size("rows")
    key = jnp.where(live_mask > 0, owner_ids[:, 0], -1)
    extra = jnp.pad(key.astype(jnp.bfloat16)[None, :], ((0, 15), (0, columns - rows_here)))
    block = jnp.concatenate([embeddings, extra], axis=0)
    held = block.shape[0]
    blocks = plane_gather(block, owners, 96, 1)
    keys = blocks[:, rows_here, :rows_here].astype(jnp.int32)
    keys = jnp.pad(keys, ((0, 0), (0, held - rows_here)), constant_values=-1).reshape(-1)
    everyone = blocks.reshape(owners * held, columns)
    share = columns // owners
    live = (keys >= 0).astype(jnp.bfloat16)[:, None]
    own = lax.dynamic_slice_in_dim(everyone, lax.axis_index("rows") * share, share, 1) * live
    part = lax.dot_general(
        own, everyone, (((0,), (0,)), ((), ())), preferred_element_type=jnp.float32
    )
    moment = plane_gather(part, owners, 32, 2, True).reshape(columns, columns)
    alive = (live_mask > 0).astype(jnp.float32)[:, None]
    return join_rows(
        embeddings, owner_ids, alive, root_of(moment), blocks, keys.reshape(owners, 1, held)
    )


def solution(mesh):
    placed = (P(("rows", "rep"), None), P(("rows", "rep"), None), P(("rows", "rep")))

    def per_device(embeddings, owner_ids, live_mask):
        gathered = embeddings.shape[0] * mesh.shape["rows"]
        fits = gathered <= JOIN_ROWS and mesh.shape["rep"] == 2
        join = by_gather if fits else by_exchange
        return join(embeddings, owner_ids, live_mask)

    return jax.shard_map(
        per_device, mesh=mesh, in_specs=placed, out_specs=P(("rows", "rep"), None), check_vma=False
    )
```

```python
import functools

import jax
import jax.numpy as jnp
from jax import lax
from jax.experimental import pallas as pl
from jax.experimental.pallas import tpu as pltpu
from jax.sharding import PartitionSpec as P

BUCKET = 1024
JOIN_ROWS = 8192
KERNEL_SCALE = 4.0
EPSILON = 1e-06
SPLIT = lax.Precision.HIGH
PRECISE = lax.Precision.HIGHEST


def block_positions(owner_block, owners, slot_cap):
    rows = owner_block.shape[0]
    same = owner_block[:, None] == owner_block[None, :]
    index = jnp.arange(rows, dtype=jnp.int32)
    earlier = index[None, :] < index[:, None]
    slot_rank = jnp.sum((same & earlier).astype(jnp.int32), axis=1)
    return owner_block * slot_cap + slot_rank


def whiten(embedded, inverse_root):
    mapped = jnp.dot(embedded, inverse_root, preferred_element_type=jnp.float32)
    return (mapped * lax.rsqrt(jnp.mean(mapped * mapped, axis=1, keepdims=True) + EPSILON)).astype(
        jnp.bfloat16
    )


def root_of(moment):
    y = moment / jnp.max(jnp.sum(jnp.abs(moment), axis=1))
    eye = jnp.eye(y.shape[0], dtype=jnp.float32)
    square = jnp.dot(y, y, precision=SPLIT)
    inner = 1.6875 * eye - 0.5625 * y + 0.0625 * square
    return (2.25 * eye - 2.4375 * y + jnp.dot(square, inner, precision=SPLIT)).astype(jnp.bfloat16)


def masked_means(queries, members, same, alive):
    scores = lax.dot_general(
        queries, members, (((1,), (1,)), ((), ())), preferred_element_type=jnp.float32
    )
    weights = jnp.where(same, jnp.exp(KERNEL_SCALE * (scores / members.shape[1] - 1.0)), 0.0)
    denominator = jnp.sum(weights, axis=1, keepdims=True)
    summed = jnp.dot(weights.astype(jnp.bfloat16), members, preferred_element_type=jnp.float32)
    averaged = summed / jnp.where(alive[:, None] > 0, denominator, 1.0)
    normed = averaged * lax.rsqrt(jnp.mean(averaged * averaged, axis=1, keepdims=True) + EPSILON)
    return (normed * alive[:, None]).astype(jnp.bfloat16)


def spread(values, positions, slots_all):
    return jnp.zeros((slots_all,) + values.shape[1:], values.dtype).at[positions].set(values)


def by_exchange(embeddings, owner_ids, live_mask):
    rows_here, columns = embeddings.shape
    owners = lax.axis_size("rows")
    slot_cap = BUCKET // owners
    positions = block_positions(owner_ids[:, 0], owners, slot_cap)
    live_rows = live_mask.astype(jnp.bfloat16)
    masked = embeddings * live_rows[:, None]
    partial_moment = lax.dot_general(
        masked, masked, (((0,), (0,)), ((), ())), preferred_element_type=jnp.float32
    )
    inverse_root = root_of(lax.psum(partial_moment, ("rows", "rep")))
    whitened = whiten(embeddings, inverse_root)

    def swapped(values):
        return lax.all_to_all(values, "rows", split_axis=0, concat_axis=0, tiled=True)

    members = swapped(
        spread(whitened, positions, BUCKET).reshape(owners, slot_cap, columns)
    ).reshape(BUCKET, columns)
    alive = swapped(spread(live_rows, positions, BUCKET).reshape(owners, slot_cap))
    alive = alive.reshape(BUCKET).astype(jnp.float32)
    means = masked_means(members, members, alive[None, :] > 0, alive)
    returned = swapped(means.reshape(owners, slot_cap, columns))
    return returned.reshape(BUCKET, columns)[positions]


def gather_kernel(owners, reduced, chunks, *refs):
    if reduced:
        x_ref, out_ref, other, own, pair_sems, here_sem, z_send, z_recv, y_send, y_recv, c_send, c_recv = refs
    else:
        x_ref, out_ref, here_sem, z_send, z_recv, y_send, y_recv, c_send, c_recv = refs
    me = lax.axis_index("rows")
    core, y, z = me % 2, (me // 2) % 2, me // 4
    depth = owners // 4

    def at(z_, y_, core_):
        return z_ * 4 + y_ * 2 + core_

    beside, sibling = at(z, 1 - y, core), at(z, y, 1 - core)
    along = [at((z + d) % depth, y, core) for d in range(1, depth)]
    barrier = pltpu.get_barrier_semaphore()
    for peer in along + [beside, sibling]:
        pl.semaphore_signal(
            barrier, inc=1, device_id={"rows": peer}, device_id_type=pl.DeviceIdType.MESH
        )
    if reduced:
        across = {"rep": 1 - lax.axis_index("rep")}
        pl.semaphore_signal(
            barrier, inc=1, device_id=across, device_id_type=pl.DeviceIdType.MESH
        )
    pl.semaphore_wait(barrier, depth + 1 + int(reduced))

    source = x_ref
    if reduced:
        swap = pltpu.make_async_remote_copy(
            src_ref=x_ref,
            dst_ref=other,
            send_sem=pair_sems.at[0],
            recv_sem=pair_sems.at[1],
            device_id=across,
            device_id_type=pl.DeviceIdType.MESH,
        )
        swap.start()
        swap.wait()
        own[...] = x_ref[...] + other[...]
        source = own

    started = []

    def send(block, k, peer, send_sems, recv_sems, n, first=False):
        rows = pl.ds(*chunks[k])
        copy = pltpu.make_async_remote_copy(
            src_ref=source.at[rows] if first else out_ref.at[block, rows],
            dst_ref=out_ref.at[block, rows],
            send_sem=send_sems.at[n, k],
            recv_sem=recv_sems.at[n, k],
            device_id={"rows": peer},
            device_id_type=pl.DeviceIdType.MESH,
        )
        copy.start()
        started.append(copy)

    def arrived(block, k, recv_sems, n):
        rows = pl.ds(*chunks[k])
        place = out_ref.at[block, rows]
        pltpu.make_async_copy(place, place, recv_sems.at[n, k]).wait()

    here = pltpu.make_async_copy(source, out_ref.at[me], here_sem)
    here.start()
    order = sorted(range(1, depth), key=lambda d: min(d, depth - d))
    for k in range(len(chunks)):
        send(me, k, beside, y_send, y_recv, 0, True)
        for d in order:
            send(me, k, along[d - 1], z_send, z_recv, d - 1, True)
        send(me, k, sibling, c_send, c_recv, 0, True)
    for k in range(len(chunks)):
        for d in order:
            block = at((z + depth - d) % depth, y, core)
            arrived(block, k, z_recv, d - 1)
            send(block, k, beside, y_send, y_recv, d)
            send(block, k, sibling, c_send, c_recv, d)
    for d in [0] + order:
        for k in range(len(chunks)):
            block = at((z + depth - d) % depth, 1 - y, core)
            arrived(block, k, y_recv, d)
            send(block, k, sibling, c_send, c_recv, depth + d)
    for d in range(depth):
        for k in range(len(chunks)):
            arrived(at((z + depth - d) % depth, y, 1 - core), k, c_recv, d)
            arrived(at((z + depth - d) % depth, 1 - y, 1 - core), k, c_recv, depth + d)
    for copy in started:
        copy.wait_send()
    here.wait()


def plane_gather(block, owners, chunk, collective_id, reduced=False):
    rows = block.shape[0]
    chunks = [(start, min(chunk, rows - start)) for start in range(0, rows, chunk)]
    n, depth = len(chunks), owners // 4
    dma = pltpu.SemaphoreType.DMA
    scratch = [dma(())] + [
        dma((count, n)) for count in (depth - 1, depth - 1, depth, depth, 2 * depth, 2 * depth)
    ]
    if reduced:
        scratch = [
            pltpu.VMEM(block.shape, block.dtype),
            pltpu.VMEM(block.shape, block.dtype),
            dma((2,)),
        ] + scratch
    return pl.pallas_call(
        functools.partial(gather_kernel, owners, reduced, chunks),
        out_shape=jax.ShapeDtypeStruct((owners,) + block.shape, block.dtype),
        in_specs=[pl.BlockSpec(memory_space=pltpu.VMEM if reduced else pl.ANY)],
        out_specs=pl.BlockSpec(memory_space=pl.ANY),
        scratch_shapes=scratch,
        compiler_params=pltpu.CompilerParams(
            collective_id=collective_id, has_side_effects=True, vmem_limit_bytes=16 << 20
        ),
    )(block)


def whitened_block(rows, root):
    mapped = jnp.dot(rows, root, preferred_element_type=jnp.float32)
    scale = lax.rsqrt(jnp.mean(mapped * mapped, axis=1, keepdims=True) + EPSILON)
    return (mapped * scale).astype(jnp.bfloat16)


def join_kernel(own_ref, named_ref, alive_ref, root_ref, x_ref, key_ref, out_ref, query, total, norm):
    step = pl.program_id(0)

    @pl.when(step == 0)
    def _():
        query[...] = whitened_block(own_ref[...], root_ref[...])
        total[...] = jnp.zeros_like(total)
        norm[...] = jnp.zeros_like(norm)

    members = whitened_block(x_ref[0], root_ref[...])
    scores = lax.dot_general(
        query[...], members, (((1,), (1,)), ((), ())), preferred_element_type=jnp.float32
    )
    close = jnp.exp(KERNEL_SCALE * (scores * (1.0 / members.shape[1]) - 1.0))
    weights = jnp.where(named_ref[...] == key_ref[0], close, 0.0)
    norm[...] += jnp.sum(weights, axis=1, keepdims=True)
    total[...] += jnp.dot(
        weights.astype(jnp.bfloat16), members, preferred_element_type=jnp.float32
    )

    @pl.when(step == pl.num_programs(0) - 1)
    def _():
        alive = alive_ref[...]
        averaged = total[...] / jnp.where(alive > 0, norm[...], 1.0)
        scale = lax.rsqrt(jnp.mean(averaged * averaged, axis=1, keepdims=True) + EPSILON)
        out_ref[...] = (averaged * scale * alive).astype(jnp.bfloat16)


def join_rows(own, named, alive, root, blocks, keys):
    rows, columns = own.shape
    count, held, _ = blocks.shape

    def whole(shape):
        return pl.BlockSpec(shape, lambda i: (0, 0))

    return pl.pallas_call(
        join_kernel,
        grid=(count,),
        out_shape=jax.ShapeDtypeStruct(own.shape, jnp.bfloat16),
        in_specs=[
            whole(own.shape),
            whole(named.shape),
            whole(alive.shape),
            whole(root.shape),
            pl.BlockSpec((1, held, columns), lambda i: (i, 0, 0)),
            pl.BlockSpec((1, 1, held), lambda i: (i, 0, 0)),
        ],
        out_specs=whole(own.shape),
        scratch_shapes=[
            pltpu.VMEM((rows, columns), jnp.bfloat16),
            pltpu.VMEM((rows, columns), jnp.float32),
            pltpu.VMEM((rows, 1), jnp.float32),
        ],
        compiler_params=pltpu.CompilerParams(vmem_limit_bytes=40 << 20),
    )(own, named, alive, root, blocks, keys)


def by_gather(embeddings, owner_ids, live_mask):
    rows_here, columns = embeddings.shape
    owners = lax.axis_size("rows")
    key = jnp.where(live_mask > 0, owner_ids[:, 0], -1)
    extra = jnp.pad(key.astype(jnp.bfloat16)[None, :], ((0, 15), (0, columns - rows_here)))
    block = jnp.concatenate([embeddings, extra], axis=0)
    held = block.shape[0]
    blocks = plane_gather(block, owners, 96, 1)
    keys = blocks[:, rows_here, :rows_here].astype(jnp.int32)
    keys = jnp.pad(keys, ((0, 0), (0, held - rows_here)), constant_values=-1).reshape(-1)
    everyone = blocks.reshape(owners * held, columns)
    share = columns // owners
    live = (keys >= 0).astype(jnp.bfloat16)[:, None]
    own = lax.dynamic_slice_in_dim(everyone, lax.axis_index("rows") * share, share, 1) * live
    part = lax.dot_general(
        own, everyone, (((0,), (0,)), ((), ())), preferred_element_type=jnp.float32
    )
    moment = plane_gather(part, owners, 32, 2, True).reshape(columns, columns)
    alive = (live_mask > 0).astype(jnp.float32)[:, None]
    return join_rows(
        embeddings, owner_ids, alive, root_of(moment), blocks.reshape(owners // 2, 2 * held, columns), keys.reshape(owners // 2, 1, 2 * held)
    )


def solution(mesh):
    placed = (P(("rows", "rep"), None), P(("rows", "rep"), None), P(("rows", "rep")))

    def per_device(embeddings, owner_ids, live_mask):
        gathered = embeddings.shape[0] * mesh.shape["rows"]
        fits = gathered <= JOIN_ROWS and mesh.shape["rep"] == 2
        join = by_gather if fits else by_exchange
        return join(embeddings, owner_ids, live_mask)

    return jax.shard_map(
        per_device, mesh=mesh, in_specs=placed, out_specs=P(("rows", "rep"), None), check_vma=False
    )
```
